32 devices in a mesh: band: 2 (over core), grow: 4 (over z), gcol: 4 (over y, x).
Axes of the slice: x: 2, y: 2, z: 4, core: 2. Of those that a mesh axis runs over, the one named last changes fastest.
Arguments:
- valence_orbitals: bfloat16 [16, 98304], replicated, may hold values from -6 to 6
- conduction_orbitals: bfloat16 [128, 98304], P(('band', 'grow', 'gcol')), may hold values from -6 to 6
- valence_energy: float32 [16], replicated, may hold values from -3 to -0.5
- conduction_energy: float32 [128], replicated, may hold values from 0.5 to 3
- coulomb_root: float32 [12288], replicated, may hold values from 0.2 to 2
- pair_bands: int32 [2, 640], P(None, ('band', 'grow', 'gcol')), may hold values from 0 to 127, as said below
- slot_counts: int32 [32], P(('band', 'grow', 'gcol')), may hold values from 1 to 19, as said below
Outputs:
- chi_zero: float32 [2, 12288, 12288], P('band', 'grow', 'gcol')
The draws below stay inside these ranges and needn't reach their ends.
Inputs may be any that keep to these rules, and one draw needn't show every extreme that they name: `pair_bands`: the slots of device d name conduction orbitals d * 4 to (d + 1) * 4 - 1 only, each of them at least once; no (valence, conduction) pair appears in two slots anywhere. `slot_counts`: the two devices of one chip (same grow and gcol index, band 0 and band 1) hold at most 20 live slots together; some chip holds exactly 20, and some device holds exactly 19.
All inputs are finite; a program needn't handle non-finite values.
Results may differ from the reference program's by a relative error of at most 0.012.
Values may be sent and summed in bfloat16 or wider, within the bound.
A program may use at most 128 MiB of HBM per device.

```python
import math
import jax
import jax.numpy as jnp
from jax import lax

N1 = 16
N2 = 24
N3 = 32
M1 = 32
M2 = 48
M3 = 64
NG = 12288
MG = 98304
VALENCE = 16
CON_DEV = 4
CONDUCTION = 128
SLOTS = 20
FREQS = 2
N_BAND = 2
N_GROW = 4
N_GCOL = 4
DEVICES = 32


def draw_pair_bands(key, part):
    key_val = jax.random.fold_in(key, 21)
    key_order = jax.random.fold_in(key, 22)
    val_keys = jax.random.split(key_val, DEVICES * CON_DEV)
    val_perms = jax.vmap(lambda k: jax.random.permutation(k, VALENCE))(val_keys).reshape(DEVICES, CON_DEV, VALENCE)
    order_keys = jax.random.split(key_order, DEVICES)
    slot_order = jax.vmap(lambda k: jax.random.permutation(k, SLOTS))(order_keys)
    drawn = jnp.arange(SLOTS).astype(jnp.int32)
    local_con = (drawn % CON_DEV)[slot_order]
    which_val = (drawn // CON_DEV)[slot_order]
    owner = jnp.arange(DEVICES).astype(jnp.int32)[:, None]
    valence = val_perms[owner, local_con, which_val]
    conduction = owner * CON_DEV + local_con
    return jnp.stack([valence.reshape(-1), conduction.reshape(-1)]).astype(jnp.int32)


def draw_slot_counts(key, part):
    chips = DEVICES // 2
    key_total = jax.random.fold_in(key, 11)
    key_first = jax.random.fold_in(key, 12)
    key_pick = jax.random.fold_in(key, 13)
    totals = jax.random.randint(key_total, (chips,), SLOTS // 2 + 1, SLOTS + 1)
    first_count = jax.random.randint(key_first, (chips,), 0, 1 << 20) % (totals - 1) + 1
    chosen = jax.random.randint(key_pick, (), 0, chips)
    is_hit = jnp.arange(chips) == chosen
    totals = jnp.where(is_hit, SLOTS, totals)
    first_count = jnp.where(is_hit, SLOTS - 1, first_count)
    return jnp.concatenate([first_count, totals - first_count]).astype(jnp.int32)


def block_scale(stream_key, dims, cuts, smallest, largest):
    level, own = 1.0, jax.random.fold_in(stream_key, 6)
    for axis_at, shards_of in cuts:
        draws = jnp.exp(jax.random.uniform(jax.random.fold_in(own, axis_at), (shards_of,), jnp.float32, smallest / len(cuts), largest / len(cuts)))
        level = level * jnp.repeat(draws, dims[axis_at] // shards_of).reshape([-1 if axis == axis_at else 1 for axis in range(len(dims))])
    return level


def noise(stream_key, extent, deviation, limit, shards=(), held_as=jnp.bfloat16):
    drawn = jax.random.normal(stream_key, extent, jnp.float32) * deviation
    if len(shards) > 0:
        drawn = block_scale(stream_key, extent, shards, -0.22, 0.18) * drawn
    return jnp.clip(drawn, min=-limit, max=limit).astype(held_as)


def setup_inputs(seed: int = 0) -> dict:
    key_of = jax.random.split(jax.random.key(seed), 8)
    valence_orbitals = noise(key_of[0], (VALENCE, MG), 1.0, 6.0)
    conduction_orbitals = noise(key_of[1], (CONDUCTION, MG), 1.0, 6.0, ((0, 32),))
    valence_energy = jnp.clip(jax.random.uniform(key_of[2], (VALENCE,), jnp.float32, -3.0, -0.5), -3.0, -0.5)
    conduction_energy = jnp.clip(jax.random.uniform(key_of[3], (CONDUCTION,), jnp.float32, 0.5, 3.0), 0.5, 3.0)
    coulomb_root = jnp.clip(jnp.exp(jax.random.uniform(key_of[4], (NG,), jnp.float32, math.log(0.2), math.log(2.0))), 0.2, 2.0)
    pair_bands = draw_pair_bands(jax.random.fold_in(key_of[7], 71), 0)
    slot_counts = draw_slot_counts(jax.random.fold_in(key_of[7], 71), 0)
    return {"valence_orbitals": valence_orbitals, "conduction_orbitals": conduction_orbitals, "valence_energy": valence_energy, "conduction_energy": conduction_energy, "coulomb_root": coulomb_root, "pair_bands": pair_bands, "slot_counts": slot_counts}


def pruned_table(keep, length):
    rows_i = lax.broadcasted_iota(jnp.int32, (keep, length), 0)
    cols_i = lax.broadcasted_iota(jnp.int32, (keep, length), 1)
    wave = (rows_i - keep // 2) % length
    angles = (wave * cols_i % length).astype(jnp.float32) * (2.0 * math.pi / length)
    return (jnp.cos(angles) + jnp.sin(angles)) / math.sqrt(length)

def reference(valence_orbitals, conduction_orbitals, valence_energy, conduction_energy, coulomb_root, pair_bands, slot_counts):
    highest = lax.Precision.HIGHEST
    total_slots = pair_bands.shape[1]
    val_index = pair_bands[0]
    con_index = pair_bands[1]
    products = valence_orbitals[val_index].astype(jnp.float32) * conduction_orbitals[con_index].astype(jnp.float32)
    lattice = products.reshape(total_slots, M1, M2, M3)
    lattice = jnp.einsum('pabc,kc->pabk', lattice, pruned_table(N3, M3), precision=highest)
    lattice = jnp.einsum('pabc,kb->pakc', lattice, pruned_table(N2, M2), precision=highest)
    lattice = jnp.einsum('pabc,ka->pkbc', lattice, pruned_table(N1, M1), precision=highest)
    density = (lattice.reshape(total_slots, N1 * N2 * N3) * coulomb_root).astype(jnp.bfloat16)
    slot_pos = (jnp.arange(total_slots) % SLOTS).astype(jnp.int32)
    is_live = slot_pos < jnp.repeat(slot_counts, SLOTS)
    energy_gap = conduction_energy[con_index] - valence_energy[val_index]
    frequency = jnp.arange(FREQS).astype(jnp.float32)[:, None]
    factor = 1.0 / math.sqrt(N_BAND * N_GROW * N_GCOL * SLOTS)
    response = 2.0 * energy_gap / (energy_gap * energy_gap + frequency * frequency)
    pair_weight = jnp.where(is_live, response, 0.0) * factor
    dense_wide = density.astype(jnp.float32)
    results = []
    for which in range(FREQS):
        weighted = (density.astype(jnp.float32) * pair_weight[which][:, None]).astype(jnp.bfloat16)
        chi_part = jnp.dot(dense_wide.T, weighted.astype(jnp.float32), precision=highest, preferred_element_type=jnp.float32)
        results.append(-chi_part)
    return jnp.stack(results)
```

```python
import functools
import math

import jax
import jax.numpy as jnp
import ml_dtypes
import numpy as np
from jax import lax
from jax.experimental import pallas as pl
from jax.experimental.pallas import tpu as pltpu
from jax.sharding import PartitionSpec as P

N1 = 16
N2 = 24
N3 = 32
M1 = 32
M2 = 48
M3 = 64
SLOTS = 20
FREQS = 2
LANES = 128
MESH = pl.DeviceIdType.MESH


def pruned_table(keep, length):
    wave = (np.arange(keep)[:, None] - keep // 2) % length
    angles = (wave * np.arange(length)[None, :] % length) * (2.0 * math.pi / length)
    return (np.cos(angles) + np.sin(angles)) / math.sqrt(length)


def density_kernel(count, val_ref, con_ref, v_ref, c_ref, first_ref, rest_ref, root_ref, out_ref, prod, mid):
    slot = pl.program_id(0)
    rows = pl.ds(pl.multiple_of(slot * M1, M1), M1)
    prod[rows, :] = (v_ref[0].astype(jnp.float32) * c_ref[0].astype(jnp.float32)).astype(jnp.bfloat16)

    @pl.when(slot == count - 1)
    def _():
        plane = M2 * M3
        step = 512
        for at in range(0, plane, step):
            mid[:, at : at + step] = jnp.dot(
                first_ref[...], prod[:, at : at + step], preferred_element_type=jnp.float32
            ).astype(jnp.bfloat16)
        kept = N2 * N3
        step = 256
        for at in range(0, kept, step):
            full = jnp.dot(mid[...], rest_ref[:, at : at + step], preferred_element_type=jnp.float32)
            full = full.reshape(count, N1, step) * root_ref[:, at : at + step][None]
            out_ref[:, :, at : at + step] = full.astype(jnp.bfloat16)


def densities(valence, conduction, coulomb_root, val_index, con_index):
    count = val_index.shape[0]
    plane = M2 * M3
    kept = N2 * N3
    first = np.kron(np.eye(count), pruned_table(N1, M1)).astype(ml_dtypes.bfloat16)
    rest = np.kron(pruned_table(N2, M2), pruned_table(N3, M3)).T.astype(ml_dtypes.bfloat16)
    whole = lambda shape: pl.BlockSpec(shape, lambda p, v, c: (0,) * len(shape))
    return pl.pallas_call(
        functools.partial(density_kernel, count),
        out_shape=jax.ShapeDtypeStruct((count, N1, kept), jnp.bfloat16),
        grid_spec=pltpu.PrefetchScalarGridSpec(
            num_scalar_prefetch=2,
            grid=(count,),
            in_specs=[
                pl.BlockSpec((1, M1, plane), lambda p, v, c: (v[p], 0, 0)),
                pl.BlockSpec((1, M1, plane), lambda p, v, c: (c[p], 0, 0)),
                whole((count * N1, count * M1)),
                whole((plane, kept)),
                whole((N1, kept)),
            ],
            out_specs=whole((count, N1, kept)),
            scratch_shapes=[
                pltpu.VMEM((count * M1, plane), jnp.bfloat16),
                pltpu.VMEM((count * N1, plane), jnp.bfloat16),
            ],
        ),
        compiler_params=pltpu.CompilerParams(vmem_limit_bytes=40 * 2**20),
        name="pair_density",
    )(
        val_index,
        con_index,
        valence,
        conduction,
        jnp.asarray(first),
        jnp.asarray(rest),
        coulomb_root.reshape(N1, kept),
    )


def exchange_kernel(
    grow, gcol, rows_in, cols_in, rows, cols,
    local_sem, r1s, r1r, c1s, c1r, r2s, r2r, c2s, c2r, r3s, r3r, c3s, c3r,
):
    b = lax.axis_index("band")
    g = lax.axis_index("grow")
    c = lax.axis_index("gcol")
    sibling = (1 - b, g, c)
    near_g = [(g + i) % grow for i in range(grow)]
    near_c = [(c + i) % gcol for i in range(gcol)]
    back_g = [(g + grow - i) % grow for i in range(grow)]
    back_c = [(c + gcol - i) % gcol for i in range(gcol)]

    barrier = pltpu.get_barrier_semaphore()
    pl.semaphore_signal(barrier, inc=1, device_id=sibling, device_id_type=MESH)
    for i in range(1, grow):
        pl.semaphore_signal(barrier, inc=1, device_id=(b, near_g[i], c), device_id_type=MESH)
    for i in range(1, gcol):
        pl.semaphore_signal(barrier, inc=1, device_id=(b, g, near_c[i]), device_id_type=MESH)
    own_row = pltpu.make_async_copy(rows_in.at[g], rows.at[b, c, g], local_sem.at[0])
    own_col = pltpu.make_async_copy(cols_in.at[c], cols.at[b, c, g], local_sem.at[1])
    own_row.start()
    own_col.start()
    pl.semaphore_wait(barrier, grow + gcol - 1)

    sent = []

    def send(src, dst, send_sem, recv_sem, target):
        copy = pltpu.make_async_remote_copy(
            src_ref=src, dst_ref=dst, send_sem=send_sem, recv_sem=recv_sem,
            device_id=target, device_id_type=MESH,
        )
        copy.start()
        sent.append(copy)

    def arrive(ref, send_sem, recv_sem):
        pltpu.make_async_remote_copy(
            src_ref=ref, dst_ref=ref, send_sem=send_sem, recv_sem=recv_sem,
            device_id=sibling, device_id_type=MESH,
        ).wait_recv()

    for i in range(1, gcol):
        send(cols_in.at[near_c[i]], cols.at[b, c, g], c1s.at[i], c1r.at[i], (b, g, near_c[i]))
    for i in range(1, grow):
        send(rows_in.at[near_g[i]], rows.at[b, c, g], r1s.at[i], r1r.at[i], (b, near_g[i], c))

    own_col.wait()
    for i in range(1, gcol):
        arrive(cols.at[b, back_c[i], g], c1s.at[i], c1r.at[i])
    block = cols.at[b, :, g]
    for i in range(1, grow):
        send(block, block, c2s.at[i], c2r.at[i], (b, near_g[i], c))
    send(block, block, c3s.at[0], c3r.at[0], sibling)

    own_row.wait()
    for i in range(1, grow):
        arrive(rows.at[b, c, back_g[i]], r1s.at[i], r1r.at[i])
    block = rows.at[b, c]
    for i in range(1, gcol):
        send(block, block, r2s.at[i], r2r.at[i], (b, g, near_c[i]))
    send(block, block, r3s.at[0], r3r.at[0], sibling)

    for i in range(1, gcol):
        block = rows.at[b, back_c[i]]
        arrive(block, r2s.at[i], r2r.at[i])
        send(block, block, r3s.at[i], r3r.at[i], sibling)
    for i in range(1, grow):
        block = cols.at[b, :, back_g[i]]
        arrive(block, c2s.at[i], c2r.at[i])
        send(block, block, c3s.at[i], c3r.at[i], sibling)
    for i in range(gcol):
        arrive(rows.at[1 - b, back_c[i]], r3s.at[i], r3r.at[i])
    for i in range(grow):
        arrive(cols.at[1 - b, :, back_g[i]], c3s.at[i], c3r.at[i])
    for copy in sent:
        copy.wait_send()


def exchange(rows_in, cols_in, grow, gcol):
    sem = lambda n: pltpu.SemaphoreType.DMA((n,))
    return pl.pallas_call(
        functools.partial(exchange_kernel, grow, gcol),
        out_shape=(
            jax.ShapeDtypeStruct((2, gcol, grow) + rows_in.shape[1:], rows_in.dtype),
            jax.ShapeDtypeStruct((2, gcol, grow) + cols_in.shape[1:], cols_in.dtype),
        ),
        in_specs=[pl.BlockSpec(memory_space=pl.ANY)] * 2,
        out_specs=(pl.BlockSpec(memory_space=pl.ANY),) * 2,
        scratch_shapes=[sem(2)]
        + [sem(grow)] * 2 + [sem(gcol)] * 2
        + [sem(gcol)] * 2 + [sem(grow)] * 2
        + [sem(gcol)] * 2 + [sem(grow)] * 2,
        compiler_params=pltpu.CompilerParams(collective_id=0, has_side_effects=True),
        name="panel_exchange",
    )(rows_in, cols_in)


def per_device(
    valence_orbitals,
    conduction_orbitals,
    valence_energy,
    conduction_energy,
    coulomb_root,
    pair_bands,
    slot_counts,
):
    grow_size = lax.axis_size("grow")
    gcol_size = lax.axis_size("gcol")
    chips = grow_size * gcol_size
    factor = 1.0 / math.sqrt(2 * chips * SLOTS)
    local_slots = pair_bands.shape[1]
    held_con = conduction_orbitals.shape[0]
    half_slots = local_slots // 2
    band_rank = lax.axis_index("band")

    valence = valence_orbitals.reshape(-1, M1, M2 * M3)
    both_con = lax.all_gather(
        conduction_orbitals.reshape(held_con, M1, M2 * M3), "band", axis=0, tiled=True
    )
    facts = jnp.concatenate([pair_bands.reshape(-1), slot_counts])
    facts = lax.all_gather(facts, ("band", "grow", "gcol"), axis=0, tiled=False)
    facts = facts.reshape(2, chips, -1)
    lists = facts[:, :, : 2 * local_slots].reshape(2, chips, 2, local_slots)
    counts = facts[:, :, 2 * local_slots]
    position = jnp.arange(local_slots)[None, :]
    first_count = counts[0][:, None]
    source = jnp.where(position < first_count, position, local_slots + position - first_count)
    source = jnp.minimum(source, 2 * local_slots - 1)
    is_live = position < first_count + counts[1][:, None]
    chip_lists = lists.transpose(2, 1, 0, 3).reshape(2, chips, 2 * local_slots)
    val_all = jnp.take_along_axis(chip_lists[0], source, axis=1)
    con_all = jnp.take_along_axis(chip_lists[1], source, axis=1)
    local_all = con_all % held_con + source // local_slots * held_con

    my_chip = lax.axis_index("grow") * gcol_size + lax.axis_index("gcol")
    mine = lambda x: lax.dynamic_slice(x, (my_chip, band_rank * half_slots), (1, half_slots))[0]
    density = densities(valence, both_con, coulomb_root, mine(val_all), mine(local_all))

    row_block = N1 * N2 * N3 // grow_size
    col_block = N1 * N2 * N3 // gcol_size

    def wire(blocks, block):
        parts = density.reshape(half_slots, blocks, block // LANES, LANES).transpose(1, 0, 2, 3)
        return parts.reshape(blocks, half_slots * (block // LANES), LANES)

    row_panel, col_panel = exchange(
        wire(grow_size, row_block), wire(gcol_size, col_block), grow_size, gcol_size
    )
    row_panel = row_panel.reshape(2 * chips * half_slots, row_block)
    col_panel = col_panel.reshape(2 * chips * half_slots, col_block)

    gap = conduction_energy[con_all] - valence_energy[val_all]
    frequency = band_rank.astype(jnp.float32)
    weight = jnp.where(is_live, 2.0 * gap / (gap * gap + frequency * frequency), 0.0) * factor
    weight = weight.reshape(grow_size, gcol_size, 2, half_slots).transpose(2, 1, 0, 3).reshape(-1, 1)
    weighted = (col_panel.astype(jnp.float32) * -weight).astype(jnp.bfloat16)
    chi = lax.dot_general(
        row_panel, weighted, (((0,), (0,)), ((), ())), preferred_element_type=jnp.float32
    )
    return chi[None]


def solution(mesh):
    return jax.shard_map(
        per_device,
        mesh=mesh,
        in_specs=(
            P(),
            P(("band", "grow", "gcol"), None),
            P(),
            P(),
            P(),
            P(None, ("band", "grow", "gcol")),
            P(("band", "grow", "gcol")),
        ),
        out_specs=P("band", "grow", "gcol"),
        check_vma=False,
    )
```

```python
import functools
import math

import jax
import jax.numpy as jnp
import ml_dtypes
import numpy as np
from jax import lax
from jax.experimental import pallas as pl
from jax.experimental.pallas import tpu as pltpu
from jax.sharding import PartitionSpec as P

N1 = 16
N2 = 24
N3 = 32
M1 = 32
M2 = 48
M3 = 64
SLOTS = 20
FREQS = 2
LANES = 128
WEIGHT_ROWS = 16
MESH = pl.DeviceIdType.MESH


def pruned_table(keep, length):
    wave = (np.arange(keep)[:, None] - keep // 2) % length
    angles = (wave * np.arange(length)[None, :] % length) * (2.0 * math.pi / length)
    return (np.cos(angles) + np.sin(angles)) / math.sqrt(length)


def pick_slot(p, own, other, band, held_con):
    slots = (own.shape[0] - 1) // 2
    b = band[0]
    is_first = b == 0
    first = jnp.where(is_first, own[2 * slots], other[2 * slots])
    total = own[2 * slots] + other[2 * slots]
    position = b * (slots // 2) + p
    in_first = position < first
    column = jnp.where(in_first, position, jnp.minimum(position - first, slots - 1))
    is_own = in_first == is_first
    val = jnp.where(is_own, own[column], other[column])
    con = jnp.where(is_own, own[slots + column], other[slots + column])
    return val, con, con % held_con, is_own, position < total


def density_kernel(
    count, held_con, factor, own, other, band, val_energy, con_energy,
    v_ref, own_ref, other_ref, first_ref, rest_ref, root_ref, out_ref, weight_ref, prod, mid,
):
    slot = pl.program_id(0)
    val, con, _, is_own, live = pick_slot(slot, own, other, band, held_con)

    @pl.when(slot == 0)
    def _():
        weight_ref[...] = jnp.zeros_like(weight_ref)

    gap = jnp.full((1, LANES), con_energy[con] - val_energy[val], jnp.float32)
    keep = jnp.where(live, -factor, 0.0)
    for f in range(FREQS):
        response = 2.0 * gap / (gap * gap + float(f * f))
        weight_ref[f, pl.ds(slot, 1), :] = response * keep

    rows = pl.ds(pl.multiple_of(slot * M1, M1), M1)

    @pl.when(is_own)
    def _():
        prod[rows, :] = (v_ref[0].astype(jnp.float32) * own_ref[0].astype(jnp.float32)).astype(jnp.bfloat16)

    @pl.when(jnp.logical_not(is_own))
    def _():
        prod[rows, :] = (v_ref[0].astype(jnp.float32) * other_ref[0].astype(jnp.float32)).astype(jnp.bfloat16)

    @pl.when(slot == count - 1)
    def _():
        plane = M2 * M3
        step = 512
        for at in range(0, plane, step):
            mid[:, at : at + step] = jnp.dot(
                first_ref[...], prod[:, at : at + step], preferred_element_type=jnp.float32
            ).astype(jnp.bfloat16)
        kept = N2 * N3
        step = 256
        for at in range(0, kept, step):
            full = jnp.dot(mid[...], rest_ref[:, at : at + step], preferred_element_type=jnp.float32)
            full = full.reshape(count, N1, step) * root_ref[:, at : at + step][None]
            out_ref[:, :, at : at + step] = full.astype(jnp.bfloat16)


def densities(valence, con_own, con_other, coulomb_root, own, other, band, val_energy, con_energy, factor):
    count = (own.shape[0] - 1) // 4
    held_con = con_own.shape[0]
    plane = M2 * M3
    kept = N2 * N3
    first = np.kron(np.eye(count), pruned_table(N1, M1)).astype(ml_dtypes.bfloat16)
    rest = np.kron(pruned_table(N2, M2), pruned_table(N3, M3)).T.astype(ml_dtypes.bfloat16)
    whole = lambda shape: pl.BlockSpec(shape, lambda p, *_: (0,) * len(shape))
    choose = lambda at: lambda p, o, t, b, ve, ce: (pick_slot(p, o, t, b, held_con)[at], 0, 0)
    return pl.pallas_call(
        functools.partial(density_kernel, count, held_con, factor),
        out_shape=(
            jax.ShapeDtypeStruct((count, N1, kept), jnp.bfloat16),
            jax.ShapeDtypeStruct((FREQS, WEIGHT_ROWS, LANES), jnp.float32),
        ),
        grid_spec=pltpu.PrefetchScalarGridSpec(
            num_scalar_prefetch=5,
            grid=(count,),
            in_specs=[
                pl.BlockSpec((1, M1, plane), choose(0)),
                pl.BlockSpec((1, M1, plane), choose(2)),
                pl.BlockSpec((1, M1, plane), choose(2)),
                whole((count * N1, count * M1)),
                whole((plane, kept)),
                whole((N1, kept)),
            ],
            out_specs=(whole((count, N1, kept)), whole((FREQS, WEIGHT_ROWS, LANES))),
            scratch_shapes=[
                pltpu.VMEM((count * M1, plane), jnp.bfloat16),
                pltpu.VMEM((count * N1, plane), jnp.bfloat16),
            ],
        ),
        compiler_params=pltpu.CompilerParams(vmem_limit_bytes=40 * 2**20),
        name="pair_density",
    )(
        own, other, band, val_energy, con_energy,
        valence, con_own, con_other,
        jnp.asarray(first), jnp.asarray(rest), coulomb_root.reshape(N1, kept),
    )


def exchange_kernel(
    grow, gcol, rows_in, cols_in, weights_in, rows, cols, weights,
    local_sem, r1s, r1r, c1s, c1r, r2s, r2r, c2s, c2r, r3s, r3r, c3s, c3r, w1s, w1r, w2s, w2r, w3s, w3r,
):
    b = lax.axis_index("band")
    g = lax.axis_index("grow")
    c = lax.axis_index("gcol")
    sibling = (1 - b, g, c)
    near_g = [(g + i) % grow for i in range(grow)]
    near_c = [(c + i) % gcol for i in range(gcol)]
    back_g = [(g + grow - i) % grow for i in range(grow)]
    back_c = [(c + gcol - i) % gcol for i in range(gcol)]

    barrier = pltpu.get_barrier_semaphore()
    pl.semaphore_signal(barrier, inc=1, device_id=sibling, device_id_type=MESH)
    for i in range(1, grow):
        pl.semaphore_signal(barrier, inc=1, device_id=(b, near_g[i], c), device_id_type=MESH)
    for i in range(1, gcol):
        pl.semaphore_signal(barrier, inc=1, device_id=(b, g, near_c[i]), device_id_type=MESH)
    own_row = pltpu.make_async_copy(rows_in.at[g], rows.at[b, c, g], local_sem.at[0])
    own_col = pltpu.make_async_copy(cols_in.at[c], cols.at[b, c, g], local_sem.at[1])
    own_weight = pltpu.make_async_copy(weights_in, weights.at[b, c, g], local_sem.at[2])
    own_row.start()
    own_col.start()
    own_weight.start()
    pl.semaphore_wait(barrier, grow + gcol - 1)

    sent = []

    def send(src, dst, send_sem, recv_sem, target):
        copy = pltpu.make_async_remote_copy(
            src_ref=src, dst_ref=dst, send_sem=send_sem, recv_sem=recv_sem,
            device_id=target, device_id_type=MESH,
        )
        copy.start()
        sent.append(copy)

    def arrive(ref, send_sem, recv_sem):
        pltpu.make_async_remote_copy(
            src_ref=ref, dst_ref=ref, send_sem=send_sem, recv_sem=recv_sem,
            device_id=sibling, device_id_type=MESH,
        ).wait_recv()

    for i in range(1, gcol):
        send(weights_in, weights.at[b, c, g], w1s.at[i], w1r.at[i], (b, g, near_c[i]))
        send(cols_in.at[near_c[i]], cols.at[b, c, g], c1s.at[i], c1r.at[i], (b, g, near_c[i]))
    for i in range(1, grow):
        send(rows_in.at[near_g[i]], rows.at[b, c, g], r1s.at[i], r1r.at[i], (b, near_g[i], c))

    own_col.wait()
    own_weight.wait()
    for i in range(1, gcol):
        arrive(weights.at[b, back_c[i], g], w1s.at[i], w1r.at[i])
    block = weights.at[b, :, g]
    for i in range(1, grow):
        send(block, block, w2s.at[i], w2r.at[i], (b, near_g[i], c))
    send(block, block, w3s.at[0], w3r.at[0], sibling)
    for i in range(1, gcol):
        arrive(cols.at[b, back_c[i], g], c1s.at[i], c1r.at[i])
    block = cols.at[b, :, g]
    for i in range(1, grow):
        send(block, block, c2s.at[i], c2r.at[i], (b, near_g[i], c))
    send(block, block, c3s.at[0], c3r.at[0], sibling)

    own_row.wait()
    for i in range(1, grow):
        arrive(rows.at[b, c, back_g[i]], r1s.at[i], r1r.at[i])
    block = rows.at[b, c]
    for i in range(1, gcol):
        send(block, block, r2s.at[i], r2r.at[i], (b, g, near_c[i]))
    send(block, block, r3s.at[0], r3r.at[0], sibling)

    for i in range(1, gcol):
        block = rows.at[b, back_c[i]]
        arrive(block, r2s.at[i], r2r.at[i])
        send(block, block, r3s.at[i], r3r.at[i], sibling)
    for i in range(1, grow):
        block = weights.at[b, :, back_g[i]]
        arrive(block, w2s.at[i], w2r.at[i])
        send(block, block, w3s.at[i], w3r.at[i], sibling)
    for i in range(1, grow):
        block = cols.at[b, :, back_g[i]]
        arrive(block, c2s.at[i], c2r.at[i])
        send(block, block, c3s.at[i], c3r.at[i], sibling)
    for i in range(gcol):
        arrive(rows.at[1 - b, back_c[i]], r3s.at[i], r3r.at[i])
    for i in range(grow):
        arrive(weights.at[1 - b, :, back_g[i]], w3s.at[i], w3r.at[i])
        arrive(cols.at[1 - b, :, back_g[i]], c3s.at[i], c3r.at[i])
    for copy in sent:
        copy.wait_send()


def exchange(rows_in, cols_in, weights_in, grow, gcol):
    sem = lambda n: pltpu.SemaphoreType.DMA((n,))
    return pl.pallas_call(
        functools.partial(exchange_kernel, grow, gcol),
        out_shape=(
            jax.ShapeDtypeStruct((2, gcol, grow) + rows_in.shape[1:], rows_in.dtype),
            jax.ShapeDtypeStruct((2, gcol, grow) + cols_in.shape[1:], cols_in.dtype),
            jax.ShapeDtypeStruct((2, gcol, grow) + weights_in.shape, weights_in.dtype),
        ),
        in_specs=[pl.BlockSpec(memory_space=pl.ANY)] * 3,
        out_specs=(pl.BlockSpec(memory_space=pl.ANY),) * 3,
        scratch_shapes=[sem(3)]
        + [sem(grow)] * 2 + [sem(gcol)] * 2
        + [sem(gcol)] * 2 + [sem(grow)] * 2
        + [sem(gcol)] * 2 + [sem(grow)] * 2
        + [sem(gcol)] * 2 + [sem(grow)] * 2 + [sem(grow)] * 2,
        compiler_params=pltpu.CompilerParams(collective_id=0, has_side_effects=True),
        name="panel_exchange",
    )(rows_in, cols_in, weights_in)


def chi_kernel(count, tile, row_ref, col_ref, weight_ref, out_ref, lift, left, right):
    at_tile = pl.program_id(0)
    band = lax.axis_index("band")

    def unpack(panel, into, weighted):
        sources = into.shape[0] // count
        groups = into.shape[1] // LANES
        stride = count * groups
        total = sources * stride
        chunk = math.gcd(total, 512)

        def widen(s, carry):
            part = pl.ds(pl.multiple_of(s * chunk, chunk), chunk)
            lift[part, :] = panel[part, :].astype(jnp.float32)
            return carry

        lax.fori_loop(0, total // chunk, widen, 0)

        def place(p, carry):
            to = pl.ds(pl.multiple_of(p * sources, sources), sources)
            if weighted:
                scale = weight_ref[pl.ds(band * WEIGHT_ROWS + p, sources, stride=FREQS * WEIGHT_ROWS), :]
            for j in range(groups):
                piece = lift[pl.ds(p * groups + j, sources, stride=stride), :]
                if weighted:
                    piece = piece * scale
                into[to, j * LANES : (j + 1) * LANES] = piece.astype(jnp.bfloat16)
            return carry

        lax.fori_loop(0, count, place, 0)

    @pl.when(at_tile == 0)
    def _():
        unpack(row_ref, left, False)
        unpack(col_ref, right, True)

    lhs = left[:, pl.ds(pl.multiple_of(at_tile * tile, tile), tile)]
    width = right.shape[1]
    step = math.gcd(width, 1024)
    for at in range(0, width, step):
        out_ref[0, :, at : at + step] = lax.dot_general(
            lhs, right[:, at : at + step], (((0,), (0,)), ((), ())), preferred_element_type=jnp.float32
        )


def chi_block(row_panel, col_panel, weights, count, row_block, col_block):
    sources = weights.shape[0] // (FREQS * WEIGHT_ROWS)
    tile = math.gcd(row_block, 256)
    whole = lambda x: pl.BlockSpec(x.shape, lambda m: (0, 0), pipeline_mode=pl.Buffered(1))
    pairs = sources * count
    return pl.pallas_call(
        functools.partial(chi_kernel, count, tile),
        out_shape=jax.ShapeDtypeStruct((1, row_block, col_block), jnp.float32),
        grid=(row_block // tile,),
        in_specs=[whole(row_panel), whole(col_panel), whole(weights)],
        out_specs=pl.BlockSpec((1, tile, col_block), lambda m: (0, m, 0)),
        scratch_shapes=[
            pltpu.VMEM((max(row_panel.shape[0], col_panel.shape[0]), LANES), jnp.float32),
            pltpu.VMEM((pairs, row_block), jnp.bfloat16),
            pltpu.VMEM((pairs, col_block), jnp.bfloat16),
        ],
        compiler_params=pltpu.CompilerParams(vmem_limit_bytes=56 * 2**20),
        name="chi_block",
    )(row_panel, col_panel, weights)


def per_device(
    valence_orbitals,
    conduction_orbitals,
    valence_energy,
    conduction_energy,
    coulomb_root,
    pair_bands,
    slot_counts,
):
    grow_size = lax.axis_size("grow")
    gcol_size = lax.axis_size("gcol")
    factor = 1.0 / math.sqrt(2 * grow_size * gcol_size * SLOTS)
    half_slots = pair_bands.shape[1] // 2
    swap = [(0, 1), (1, 0)]

    con_own = conduction_orbitals.reshape(-1, M1, M2 * M3)
    con_other = lax.ppermute(con_own, "band", swap)
    own = jnp.concatenate([pair_bands.reshape(-1), slot_counts])
    other = lax.ppermute(own, "band", swap)
    band = lax.axis_index("band").astype(jnp.int32).reshape(1)
    density, weights = densities(
        valence_orbitals.reshape(-1, M1, M2 * M3), con_own, con_other, coulomb_root,
        own, other, band, valence_energy, conduction_energy, factor,
    )

    row_block = N1 * N2 * N3 // grow_size
    col_block = N1 * N2 * N3 // gcol_size

    def wire(blocks, block):
        parts = density.reshape(half_slots, blocks, block // LANES, LANES).transpose(1, 0, 2, 3)
        return parts.reshape(blocks, half_slots * (block // LANES), LANES)

    row_panel, col_panel, all_weights = exchange(
        wire(grow_size, row_block), wire(gcol_size, col_block), weights, grow_size, gcol_size
    )
    return chi_block(
        row_panel.reshape(-1, LANES),
        col_panel.reshape(-1, LANES),
        all_weights.reshape(-1, LANES),
        half_slots,
        row_block,
        col_block,
    )


def solution(mesh):
    return jax.shard_map(
        per_device,
        mesh=mesh,
        in_specs=(
            P(),
            P(("band", "grow", "gcol"), None),
            P(),
            P(),
            P(),
            P(None, ("band", "grow", "gcol")),
            P(("band", "grow", "gcol")),
        ),
        out_specs=P("band", "grow", "gcol"),
        check_vma=False,
    )
```

```python
import functools
import math

import jax
import jax.numpy as jnp
import ml_dtypes
import numpy as np
from jax import lax
from jax.experimental import pallas as pl
from jax.experimental.pallas import tpu as pltpu
from jax.sharding import PartitionSpec as P

N1 = 16
N2 = 24
N3 = 32
M1 = 32
M2 = 48
M3 = 64
SLOTS = 20
FREQS = 2
LANES = 128
WEIGHT_ROWS = 16
MESH = pl.DeviceIdType.MESH


def pruned_table(keep, length):
    wave = (np.arange(keep)[:, None] - keep // 2) % length
    angles = (wave * np.arange(length)[None, :] % length) * (2.0 * math.pi / length)
    return (np.cos(angles) + np.sin(angles)) / math.sqrt(length)


def pick_slot(p, own, other, band, held_con):
    slots = (own.shape[0] - 1) // 2
    b = band[0]
    is_first = b == 0
    first = jnp.where(is_first, own[2 * slots], other[2 * slots])
    total = own[2 * slots] + other[2 * slots]
    position = b * (slots // 2) + p
    in_first = position < first
    column = jnp.where(in_first, position, jnp.minimum(position - first, slots - 1))
    is_own = in_first == is_first
    val = jnp.where(is_own, own[column], other[column])
    con = jnp.where(is_own, own[slots + column], other[slots + column])
    return val, con, con % held_con, is_own, position < total


def density_kernel(
    count, held_con, factor, own, other, band, val_energy, con_energy,
    v_ref, own_ref, other_ref, first_ref, rest_ref, root_ref, out_ref, weight_ref, prod, mid,
):
    slot = pl.program_id(0)
    val, con, _, is_own, live = pick_slot(slot, own, other, band, held_con)

    @pl.when(slot == 0)
    def _():
        weight_ref[...] = jnp.zeros_like(weight_ref)

    gap = jnp.full((1, LANES), con_energy[con] - val_energy[val], jnp.float32)
    keep = jnp.where(live, -factor, 0.0)
    for f in range(FREQS):
        response = 2.0 * gap / (gap * gap + float(f * f))
        weight_ref[f, pl.ds(slot, 1), :] = response * keep

    rows = pl.ds(pl.multiple_of(slot * M1, M1), M1)

    @pl.when(is_own)
    def _():
        prod[rows, :] = (v_ref[0].astype(jnp.float32) * own_ref[0].astype(jnp.float32)).astype(jnp.bfloat16)

    @pl.when(jnp.logical_not(is_own))
    def _():
        prod[rows, :] = (v_ref[0].astype(jnp.float32) * other_ref[0].astype(jnp.float32)).astype(jnp.bfloat16)

    @pl.when(slot == count - 1)
    def _():
        plane = M2 * M3
        step = 512
        for at in range(0, plane, step):
            mid[:, at : at + step] = jnp.dot(
                first_ref[...], prod[:, at : at + step], preferred_element_type=jnp.float32
            ).astype(jnp.bfloat16)
        kept = N2 * N3
        step = 256
        for at in range(0, kept, step):
            full = jnp.dot(mid[...], rest_ref[:, at : at + step], preferred_element_type=jnp.float32)
            full = full.reshape(count, N1, step) * root_ref[:, at : at + step][None]
            out_ref[:, :, at : at + step] = full.astype(jnp.bfloat16)


def densities(valence, con_own, con_other, coulomb_root, own, other, band, val_energy, con_energy, factor):
    count = (own.shape[0] - 1) // 4
    held_con = con_own.shape[0]
    plane = M2 * M3
    kept = N2 * N3
    first = np.kron(np.eye(count), pruned_table(N1, M1)).astype(ml_dtypes.bfloat16)
    rest = np.kron(pruned_table(N2, M2), pruned_table(N3, M3)).T.astype(ml_dtypes.bfloat16)
    whole = lambda shape: pl.BlockSpec(shape, lambda p, *_: (0,) * len(shape))
    choose = lambda at: lambda p, o, t, b, ve, ce: (pick_slot(p, o, t, b, held_con)[at], 0, 0)
    return pl.pallas_call(
        functools.partial(density_kernel, count, held_con, factor),
        out_shape=(
            jax.ShapeDtypeStruct((count, N1, kept), jnp.bfloat16),
            jax.ShapeDtypeStruct((FREQS, WEIGHT_ROWS, LANES), jnp.float32),
        ),
        grid_spec=pltpu.PrefetchScalarGridSpec(
            num_scalar_prefetch=5,
            grid=(count,),
            in_specs=[
                pl.BlockSpec((1, M1, plane), choose(0)),
                pl.BlockSpec((1, M1, plane), choose(2)),
                pl.BlockSpec((1, M1, plane), choose(2)),
                whole((count * N1, count * M1)),
                whole((plane, kept)),
                whole((N1, kept)),
            ],
            out_specs=(whole((count, N1, kept)), whole((FREQS, WEIGHT_ROWS, LANES))),
            scratch_shapes=[
                pltpu.VMEM((count * M1, plane), jnp.bfloat16),
                pltpu.VMEM((count * N1, plane), jnp.bfloat16),
            ],
        ),
        compiler_params=pltpu.CompilerParams(vmem_limit_bytes=40 * 2**20),
        name="pair_density",
    )(
        own, other, band, val_energy, con_energy,
        valence, con_own, con_other,
        jnp.asarray(first), jnp.asarray(rest), coulomb_root.reshape(N1, kept),
    )


def exchange_kernel(
    grow, gcol, rows_in, cols_in, weights_in, rows, cols, weights,
    local_sem, r1s, r1r, c1s, c1r, r2s, r2r, up_s, up_r, down_s, down_r, r3s, r3r, c3s, c3r,
    w1s, w1r, w2s, w2r, w3s, w3r,
):
    b = lax.axis_index("band")
    g = lax.axis_index("grow")
    c = lax.axis_index("gcol")
    sibling = (1 - b, g, c)
    near_g = [(g + i) % grow for i in range(grow)]
    near_c = [(c + i) % gcol for i in range(gcol)]
    back_g = [(g + grow - i) % grow for i in range(grow)]
    back_c = [(c + gcol - i) % gcol for i in range(gcol)]

    barrier = pltpu.get_barrier_semaphore()
    pl.semaphore_signal(barrier, inc=1, device_id=sibling, device_id_type=MESH)
    for i in range(1, grow):
        pl.semaphore_signal(barrier, inc=1, device_id=(b, near_g[i], c), device_id_type=MESH)
    for i in range(1, gcol):
        pl.semaphore_signal(barrier, inc=1, device_id=(b, g, near_c[i]), device_id_type=MESH)
    own_row = pltpu.make_async_copy(rows_in.at[g], rows.at[b, c, g], local_sem.at[0])
    own_col = pltpu.make_async_copy(cols_in.at[c], cols.at[b, c, g], local_sem.at[1])
    own_weight = pltpu.make_async_copy(weights_in, weights.at[b, c, g], local_sem.at[2])
    own_row.start()
    own_col.start()
    own_weight.start()
    pl.semaphore_wait(barrier, grow + gcol - 1)

    sent = []

    def send(src, dst, send_sem, recv_sem, target):
        copy = pltpu.make_async_remote_copy(
            src_ref=src, dst_ref=dst, send_sem=send_sem, recv_sem=recv_sem,
            device_id=target, device_id_type=MESH,
        )
        copy.start()
        sent.append(copy)

    def arrive(ref, send_sem, recv_sem):
        pltpu.make_async_remote_copy(
            src_ref=ref, dst_ref=ref, send_sem=send_sem, recv_sem=recv_sem,
            device_id=sibling, device_id_type=MESH,
        ).wait_recv()

    on_right = g + 1 < grow
    on_left = g > 0
    guarded = []

    def send_if(condition, src, dst, send_sem, recv_sem, target):
        copy = pltpu.make_async_remote_copy(
            src_ref=src, dst_ref=dst, send_sem=send_sem, recv_sem=recv_sem,
            device_id=target, device_id_type=MESH,
        )

        @pl.when(condition)
        def _():
            copy.start()

        guarded.append((condition, copy))

    right = (b, jnp.minimum(g + 1, grow - 1), c)
    left = (b, jnp.maximum(g - 1, 0), c)

    def spread(src, owner, i):
        dst = cols.at[b, owner, g]
        send_if(on_right, src, dst, up_s.at[1, i], up_r.at[1, i], right)
        send_if(on_left, src, dst, down_s.at[1, i], down_r.at[1, i], left)
        send(src, dst, c3s.at[0, i], c3r.at[0, i], sibling)

    for i in range(1, gcol):
        send(cols_in.at[near_c[i]], cols.at[b, c, g], c1s.at[i], c1r.at[i], (b, g, near_c[i]))
    for i in range(1, grow):
        send(rows_in.at[near_g[i]], rows.at[b, c, g], r1s.at[i], r1r.at[i], (b, near_g[i], c))
    spread(cols_in.at[c], c, 0)
    for i in range(1, gcol):
        send(weights_in, weights.at[b, c, g], w1s.at[i], w1r.at[i], (b, g, near_c[i]))
    for i in range(1, gcol):
        piece = cols.at[b, back_c[i], g]
        arrive(piece, c1s.at[i], c1r.at[i])
        spread(piece, back_c[i], i)

    own_row.wait()
    for i in range(1, grow):
        arrive(rows.at[b, c, back_g[i]], r1s.at[i], r1r.at[i])
    block = rows.at[b, c]
    for i in range(1, gcol):
        send(block, block, r2s.at[i], r2r.at[i], (b, g, near_c[i]))
    send(block, block, r3s.at[0], r3r.at[0], sibling)

    own_weight.wait()
    for i in range(1, gcol):
        arrive(weights.at[b, back_c[i], g], w1s.at[i], w1r.at[i])
    block = weights.at[b, :, g]
    for i in range(1, grow):
        send(block, block, w2s.at[i], w2r.at[i], (b, near_g[i], c))
    send(block, block, w3s.at[0], w3r.at[0], sibling)

    def rows_to_sibling():
        for i in range(1, gcol):
            block = rows.at[b, back_c[i]]
            arrive(block, r2s.at[i], r2r.at[i])
            send(block, block, r3s.at[i], r3r.at[i], sibling)

    for s in range(1, grow):
        if s == grow - 1:
            rows_to_sibling()
        low = jnp.maximum(g - s, 0)
        high = jnp.minimum(g + s, grow - 1)
        for i in range(gcol):
            for has, at, S, R, onward, target, half in (
                (g >= s, low, up_s, up_r, on_right, right, 0),
                (g + s < grow, high, down_s, down_r, on_left, left, 1),
            ):
                piece = cols.at[b, back_c[i], at]

                @pl.when(has)
                def _():
                    arrive(piece, S.at[s, i], R.at[s, i])

                if s + 1 < grow:
                    send_if(
                        jnp.logical_and(has, onward), piece, piece, S.at[s + 1, i], R.at[s + 1, i], target
                    )
                send_if(has, piece, piece, c3s.at[s + half * grow, i], c3r.at[s + half * grow, i], sibling)

    for i in range(1, grow):
        block = weights.at[b, :, back_g[i]]
        arrive(block, w2s.at[i], w2r.at[i])
        send(block, block, w3s.at[i], w3r.at[i], sibling)
    for i in range(gcol):
        arrive(rows.at[1 - b, back_c[i]], r3s.at[i], r3r.at[i])
        arrive(cols.at[1 - b, back_c[i], g], c3s.at[0, i], c3r.at[0, i])
    for i in range(grow):
        arrive(weights.at[1 - b, :, back_g[i]], w3s.at[i], w3r.at[i])
    for s in range(1, grow):
        low = jnp.maximum(g - s, 0)
        high = jnp.minimum(g + s, grow - 1)
        for i in range(gcol):
            for has, at, half in ((g >= s, low, 0), (g + s < grow, high, 1)):

                @pl.when(has)
                def _():
                    arrive(cols.at[1 - b, back_c[i], at], c3s.at[s + half * grow, i], c3r.at[s + half * grow, i])

    own_col.wait()
    for copy in sent:
        copy.wait_send()
    for condition, copy in guarded:

        @pl.when(condition)
        def _():
            copy.wait_send()


def exchange(rows_in, cols_in, weights_in, grow, gcol):
    sem = lambda *n: pltpu.SemaphoreType.DMA(n)
    return pl.pallas_call(
        functools.partial(exchange_kernel, grow, gcol),
        out_shape=(
            jax.ShapeDtypeStruct((2, gcol, grow) + rows_in.shape[1:], rows_in.dtype),
            jax.ShapeDtypeStruct((2, gcol, grow) + cols_in.shape[1:], cols_in.dtype),
            jax.ShapeDtypeStruct((2, gcol, grow) + weights_in.shape, weights_in.dtype),
        ),
        in_specs=[pl.BlockSpec(memory_space=pl.ANY)] * 3,
        out_specs=(pl.BlockSpec(memory_space=pl.ANY),) * 3,
        scratch_shapes=[sem(3)]
        + [sem(grow)] * 2 + [sem(gcol)] * 2
        + [sem(gcol)] * 2 + [sem(grow, gcol)] * 4
        + [sem(gcol)] * 2 + [sem(2 * grow, gcol)] * 2
        + [sem(gcol)] * 2 + [sem(grow)] * 2 + [sem(grow)] * 2,
        compiler_params=pltpu.CompilerParams(collective_id=0, has_side_effects=True),
        name="panel_exchange",
    )(rows_in, cols_in, weights_in)


def chi_kernel(count, tile, row_ref, col_ref, weight_ref, out_ref, lift, left, right):
    at_tile = pl.program_id(0)
    band = lax.axis_index("band")

    def unpack(panel, into, weighted):
        sources = into.shape[0] // count
        groups = into.shape[1] // LANES
        stride = count * groups
        total = sources * stride
        chunk = math.gcd(total, 512)

        def widen(s, carry):
            part = pl.ds(pl.multiple_of(s * chunk, chunk), chunk)
            lift[part, :] = panel[part, :].astype(jnp.float32)
            return carry

        lax.fori_loop(0, total // chunk, widen, 0)

        def place(p, carry):
            to = pl.ds(pl.multiple_of(p * sources, sources), sources)
            if weighted:
                scale = weight_ref[pl.ds(band * WEIGHT_ROWS + p, sources, stride=FREQS * WEIGHT_ROWS), :]
            for j in range(groups):
                piece = lift[pl.ds(p * groups + j, sources, stride=stride), :]
                if weighted:
                    piece = piece * scale
                into[to, j * LANES : (j + 1) * LANES] = piece.astype(jnp.bfloat16)
            return carry

        lax.fori_loop(0, count, place, 0)

    @pl.when(at_tile == 0)
    def _():
        unpack(row_ref, left, False)
        unpack(col_ref, right, True)

    lhs = left[:, pl.ds(pl.multiple_of(at_tile * tile, tile), tile)]
    width = right.shape[1]
    step = math.gcd(width, 512)
    for at in range(0, width, step):
        out_ref[0, :, at : at + step] = lax.dot_general(
            lhs, right[:, at : at + step], (((0,), (0,)), ((), ())), preferred_element_type=jnp.float32
        )


def chi_block(row_panel, col_panel, weights, count, row_block, col_block):
    sources = weights.shape[0] // (FREQS * WEIGHT_ROWS)
    tile = math.gcd(row_block, 512)
    whole = lambda x: pl.BlockSpec(x.shape, lambda m: (0, 0), pipeline_mode=pl.Buffered(1))
    pairs = sources * count
    return pl.pallas_call(
        functools.partial(chi_kernel, count, tile),
        out_shape=jax.ShapeDtypeStruct((1, row_block, col_block), jnp.float32),
        grid=(row_block // tile,),
        in_specs=[whole(row_panel), whole(col_panel), whole(weights)],
        out_specs=pl.BlockSpec((1, tile, col_block), lambda m: (0, m, 0)),
        scratch_shapes=[
            pltpu.VMEM((max(row_panel.shape[0], col_panel.shape[0]), LANES), jnp.float32),
            pltpu.VMEM((pairs, row_block), jnp.bfloat16),
            pltpu.VMEM((pairs, col_block), jnp.bfloat16),
        ],
        compiler_params=pltpu.CompilerParams(vmem_limit_bytes=56 * 2**20),
        name="chi_block",
    )(row_panel, col_panel, weights)


def per_device(
    valence_orbitals,
    conduction_orbitals,
    valence_energy,
    conduction_energy,
    coulomb_root,
    pair_bands,
    slot_counts,
):
    grow_size = lax.axis_size("grow")
    gcol_size = lax.axis_size("gcol")
    factor = 1.0 / math.sqrt(2 * grow_size * gcol_size * SLOTS)
    half_slots = pair_bands.shape[1] // 2
    swap = [(0, 1), (1, 0)]

    con_own = conduction_orbitals.reshape(-1, M1, M2 * M3)
    con_other = lax.ppermute(con_own, "band", swap)
    own = jnp.concatenate([pair_bands.reshape(-1), slot_counts])
    other = lax.ppermute(own, "band", swap)
    band = lax.axis_index("band").astype(jnp.int32).reshape(1)
    density, weights = densities(
        valence_orbitals.reshape(-1, M1, M2 * M3), con_own, con_other, coulomb_root,
        own, other, band, valence_energy, conduction_energy, factor,
    )

    row_block = N1 * N2 * N3 // grow_size
    col_block = N1 * N2 * N3 // gcol_size

    def wire(blocks, block):
        parts = density.reshape(half_slots, blocks, block // LANES, LANES).transpose(1, 0, 2, 3)
        return parts.reshape(blocks, half_slots * (block // LANES), LANES)

    row_panel, col_panel, all_weights = exchange(
        wire(grow_size, row_block), wire(gcol_size, col_block), weights, grow_size, gcol_size
    )
    return chi_block(
        row_panel.reshape(-1, LANES),
        col_panel.reshape(-1, LANES),
        all_weights.reshape(-1, LANES),
        half_slots,
        row_block,
        col_block,
    )


def solution(mesh):
    return jax.shard_map(
        per_device,
        mesh=mesh,
        in_specs=(
            P(),
            P(("band", "grow", "gcol"), None),
            P(),
            P(),
            P(),
            P(None, ("band", "grow", "gcol")),
            P(("band", "grow", "gcol")),
        ),
        out_specs=P("band", "grow", "gcol"),
        check_vma=False,
    )
```

```python
import functools
import math

import jax
import jax.numpy as jnp
import ml_dtypes
import numpy as np
from jax import lax
from jax.experimental import pallas as pl
from jax.experimental.pallas import tpu as pltpu
from jax.sharding import PartitionSpec as P

N1 = 16
N2 = 24
N3 = 32
M1 = 32
M2 = 48
M3 = 64
SLOTS = 20
FREQS = 2
LANES = 128
WEIGHT_ROWS = 16
MESH = pl.DeviceIdType.MESH


def pruned_table(keep, length):
    wave = (np.arange(keep)[:, None] - keep // 2) % length
    angles = (wave * np.arange(length)[None, :] % length) * (2.0 * math.pi / length)
    return (np.cos(angles) + np.sin(angles)) / math.sqrt(length)


def pick_slot(p, own, other, band, held_con):
    slots = (own.shape[0] - 1) // 2
    b = band[0]
    is_first = b == 0
    first = jnp.where(is_first, own[2 * slots], other[2 * slots])
    total = own[2 * slots] + other[2 * slots]
    position = b * (slots // 2) + p
    in_first = position < first
    column = jnp.where(in_first, position, jnp.minimum(position - first, slots - 1))
    is_own = in_first == is_first
    val = jnp.where(is_own, own[column], other[column])
    con = jnp.where(is_own, own[slots + column], other[slots + column])
    return val, con, con % held_con, is_own, position < total


def density_kernel(
    count, held_con, factor, own, other, band, val_energy, con_energy,
    v_ref, own_ref, other_ref, first_ref, rest_ref, root_ref, out_ref, weight_ref, prod, mid,
):
    slot = pl.program_id(0)
    val, con, _, is_own, live = pick_slot(slot, own, other, band, held_con)

    @pl.when(slot == 0)
    def _():
        weight_ref[...] = jnp.zeros_like(weight_ref)

    gap = jnp.full((1, LANES), con_energy[con] - val_energy[val], jnp.float32)
    keep = jnp.where(live, -factor, 0.0)
    for f in range(FREQS):
        response = 2.0 * gap / (gap * gap + float(f * f))
        weight_ref[f, pl.ds(slot, 1), :] = response * keep

    rows = pl.ds(pl.multiple_of(slot * M1, M1), M1)

    @pl.when(is_own)
    def _():
        prod[rows, :] = (v_ref[0].astype(jnp.float32) * own_ref[0].astype(jnp.float32)).astype(jnp.bfloat16)

    @pl.when(jnp.logical_not(is_own))
    def _():
        prod[rows, :] = (v_ref[0].astype(jnp.float32) * other_ref[0].astype(jnp.float32)).astype(jnp.bfloat16)

    @pl.when(slot == count - 1)
    def _():
        plane = M2 * M3
        step = 512
        for at in range(0, plane, step):
            mid[:, at : at + step] = jnp.dot(
                first_ref[...], prod[:, at : at + step], preferred_element_type=jnp.float32
            ).astype(jnp.bfloat16)
        kept = N2 * N3
        step = 256
        for at in range(0, kept, step):
            full = jnp.dot(mid[...], rest_ref[:, at : at + step], preferred_element_type=jnp.float32)
            full = full.reshape(count, N1, step) * root_ref[:, at : at + step][None]
            out_ref[:, :, at : at + step] = full.astype(jnp.bfloat16)


def densities(valence, con_own, con_other, coulomb_root, own, other, band, val_energy, con_energy, factor):
    count = (own.shape[0] - 1) // 4
    held_con = con_own.shape[0]
    plane = M2 * M3
    kept = N2 * N3
    first = np.kron(np.eye(count), pruned_table(N1, M1)).astype(ml_dtypes.bfloat16)
    rest = np.kron(pruned_table(N2, M2), pruned_table(N3, M3)).T.astype(ml_dtypes.bfloat16)
    whole = lambda shape: pl.BlockSpec(shape, lambda p, *_: (0,) * len(shape))
    choose = lambda at: lambda p, o, t, b, ve, ce: (pick_slot(p, o, t, b, held_con)[at], 0, 0)
    return pl.pallas_call(
        functools.partial(density_kernel, count, held_con, factor),
        out_shape=(
            jax.ShapeDtypeStruct((count, N1, kept), jnp.bfloat16),
            jax.ShapeDtypeStruct((FREQS, WEIGHT_ROWS, LANES), jnp.float32),
        ),
        grid_spec=pltpu.PrefetchScalarGridSpec(
            num_scalar_prefetch=5,
            grid=(count,),
            in_specs=[
                pl.BlockSpec((1, M1, plane), choose(0)),
                pl.BlockSpec((1, M1, plane), choose(2)),
                pl.BlockSpec((1, M1, plane), choose(2)),
                whole((count * N1, count * M1)),
                whole((plane, kept)),
                whole((N1, kept)),
            ],
            out_specs=(whole((count, N1, kept)), whole((FREQS, WEIGHT_ROWS, LANES))),
            scratch_shapes=[
                pltpu.VMEM((count * M1, plane), jnp.bfloat16),
                pltpu.VMEM((count * N1, plane), jnp.bfloat16),
            ],
        ),
        compiler_params=pltpu.CompilerParams(vmem_limit_bytes=40 * 2**20),
        name="pair_density",
    )(
        own, other, band, val_energy, con_energy,
        valence, con_own, con_other,
        jnp.asarray(first), jnp.asarray(rest), coulomb_root.reshape(N1, kept),
    )


def exchange_kernel(
    grow, gcol, rows_in, cols_in, weights_in, rows, cols, weights,
    local_sem, r1s, r1r, c1s, c1r, r2s, r2r, up_s, up_r, down_s, down_r, r3s, r3r, c3s, c3r,
    w1s, w1r, w2s, w2r, w3s, w3r,
):
    b = lax.axis_index("band")
    g = lax.axis_index("grow")
    c = lax.axis_index("gcol")
    sibling = (1 - b, g, c)
    near_g = [(g + i) % grow for i in range(grow)]
    near_c = [(c + i) % gcol for i in range(gcol)]
    back_g = [(g + grow - i) % grow for i in range(grow)]
    back_c = [(c + gcol - i) % gcol for i in range(gcol)]

    barrier = pltpu.get_barrier_semaphore()
    pl.semaphore_signal(barrier, inc=1, device_id=sibling, device_id_type=MESH)
    for i in range(1, grow):
        pl.semaphore_signal(barrier, inc=1, device_id=(b, near_g[i], c), device_id_type=MESH)
    for i in range(1, gcol):
        pl.semaphore_signal(barrier, inc=1, device_id=(b, g, near_c[i]), device_id_type=MESH)
    own_row = pltpu.make_async_copy(rows_in.at[g], rows.at[b, c, g], local_sem.at[0])
    own_col = pltpu.make_async_copy(cols_in.at[c], cols.at[b, c, g], local_sem.at[1])
    own_weight = pltpu.make_async_copy(weights_in, weights.at[b, c, g], local_sem.at[2])
    own_row.start()
    own_col.start()
    own_weight.start()
    pl.semaphore_wait(barrier, grow + gcol - 1)

    sent = []

    def send(src, dst, send_sem, recv_sem, target):
        copy = pltpu.make_async_remote_copy(
            src_ref=src, dst_ref=dst, send_sem=send_sem, recv_sem=recv_sem,
            device_id=target, device_id_type=MESH,
        )
        copy.start()
        sent.append(copy)

    def arrive(ref, send_sem, recv_sem):
        pltpu.make_async_remote_copy(
            src_ref=ref, dst_ref=ref, send_sem=send_sem, recv_sem=recv_sem,
            device_id=sibling, device_id_type=MESH,
        ).wait_recv()

    on_right = g + 1 < grow
    on_left = g > 0
    guarded = []

    def send_if(condition, src, dst, send_sem, recv_sem, target):
        copy = pltpu.make_async_remote_copy(
            src_ref=src, dst_ref=dst, send_sem=send_sem, recv_sem=recv_sem,
            device_id=target, device_id_type=MESH,
        )

        @pl.when(condition)
        def _():
            copy.start()

        guarded.append((condition, copy))

    right = (b, jnp.minimum(g + 1, grow - 1), c)
    left = (b, jnp.maximum(g - 1, 0), c)

    def spread(src, owner, i):
        dst = cols.at[b, owner, g]
        send_if(on_right, src, dst, up_s.at[1, i], up_r.at[1, i], right)
        send_if(on_left, src, dst, down_s.at[1, i], down_r.at[1, i], left)
        send(src, dst, c3s.at[0, i], c3r.at[0, i], sibling)

    spread(cols_in.at[c], c, 0)
    for i in range(1, gcol):
        send(cols_in.at[near_c[i]], cols.at[b, c, g], c1s.at[i], c1r.at[i], (b, g, near_c[i]))
    for i in range(1, grow):
        send(rows_in.at[near_g[i]], rows.at[b, c, g], r1s.at[i], r1r.at[i], (b, near_g[i], c))
    for i in range(1, gcol):
        send(weights_in, weights.at[b, c, g], w1s.at[i], w1r.at[i], (b, g, near_c[i]))
    for i in range(1, gcol):
        piece = cols.at[b, back_c[i], g]
        arrive(piece, c1s.at[i], c1r.at[i])
        spread(piece, back_c[i], i)

    own_weight.wait()
    for i in range(1, gcol):
        arrive(weights.at[b, back_c[i], g], w1s.at[i], w1r.at[i])
    block = weights.at[b, :, g]
    for i in range(1, grow):
        send(block, block, w2s.at[i], w2r.at[i], (b, near_g[i], c))
    send(block, block, w3s.at[0], w3r.at[0], sibling)

    def rows_across():
        own_row.wait()
        for i in range(1, grow):
            arrive(rows.at[b, c, back_g[i]], r1s.at[i], r1r.at[i])
        block = rows.at[b, c]
        for i in range(1, gcol):
            send(block, block, r2s.at[i], r2r.at[i], (b, g, near_c[i]))
        send(block, block, r3s.at[0], r3r.at[0], sibling)

    def rows_to_sibling():
        for i in range(1, gcol):
            block = rows.at[b, back_c[i]]
            arrive(block, r2s.at[i], r2r.at[i])
            send(block, block, r3s.at[i], r3r.at[i], sibling)

    for s in range(1, grow):
        if s == grow - 1:
            rows_to_sibling()
        low = jnp.maximum(g - s, 0)
        high = jnp.minimum(g + s, grow - 1)
        for i in range(gcol):
            if s == 1 and i == 1:
                rows_across()
            for has, at, S, R, onward, target, half in (
                (g >= s, low, up_s, up_r, on_right, right, 0),
                (g + s < grow, high, down_s, down_r, on_left, left, 1),
            ):
                piece = cols.at[b, back_c[i], at]

                @pl.when(has)
                def _():
                    arrive(piece, S.at[s, i], R.at[s, i])

                if s + 1 < grow:
                    send_if(
                        jnp.logical_and(has, onward), piece, piece, S.at[s + 1, i], R.at[s + 1, i], target
                    )
                send_if(has, piece, piece, c3s.at[s + half * grow, i], c3r.at[s + half * grow, i], sibling)

    for i in range(1, grow):
        block = weights.at[b, :, back_g[i]]
        arrive(block, w2s.at[i], w2r.at[i])
        send(block, block, w3s.at[i], w3r.at[i], sibling)
    for i in range(gcol):
        arrive(rows.at[1 - b, back_c[i]], r3s.at[i], r3r.at[i])
        arrive(cols.at[1 - b, back_c[i], g], c3s.at[0, i], c3r.at[0, i])
    for i in range(grow):
        arrive(weights.at[1 - b, :, back_g[i]], w3s.at[i], w3r.at[i])
    for s in range(1, grow):
        low = jnp.maximum(g - s, 0)
        high = jnp.minimum(g + s, grow - 1)
        for i in range(gcol):
            for has, at, half in ((g >= s, low, 0), (g + s < grow, high, 1)):

                @pl.when(has)
                def _():
                    arrive(cols.at[1 - b, back_c[i], at], c3s.at[s + half * grow, i], c3r.at[s + half * grow, i])

    own_col.wait()
    for copy in sent:
        copy.wait_send()
    for condition, copy in guarded:

        @pl.when(condition)
        def _():
            copy.wait_send()


def exchange(rows_in, cols_in, weights_in, grow, gcol):
    sem = lambda *n: pltpu.SemaphoreType.DMA(n)
    return pl.pallas_call(
        functools.partial(exchange_kernel, grow, gcol),
        out_shape=(
            jax.ShapeDtypeStruct((2, gcol, grow) + rows_in.shape[1:], rows_in.dtype),
            jax.ShapeDtypeStruct((2, gcol, grow) + cols_in.shape[1:], cols_in.dtype),
            jax.ShapeDtypeStruct((2, gcol, grow) + weights_in.shape, weights_in.dtype),
        ),
        in_specs=[pl.BlockSpec(memory_space=pl.ANY)] * 3,
        out_specs=(pl.BlockSpec(memory_space=pl.ANY),) * 3,
        scratch_shapes=[sem(3)]
        + [sem(grow)] * 2 + [sem(gcol)] * 2
        + [sem(gcol)] * 2 + [sem(grow, gcol)] * 4
        + [sem(gcol)] * 2 + [sem(2 * grow, gcol)] * 2
        + [sem(gcol)] * 2 + [sem(grow)] * 2 + [sem(grow)] * 2,
        compiler_params=pltpu.CompilerParams(collective_id=0, has_side_effects=True),
        name="panel_exchange",
    )(rows_in, cols_in, weights_in)


def chi_kernel(count, tile, row_ref, col_ref, weight_ref, out_ref, lift, left, right):
    at_tile = pl.program_id(0)
    band = lax.axis_index("band")

    def unpack(panel, into, weighted):
        sources = into.shape[0] // count
        groups = into.shape[1] // LANES
        stride = count * groups
        total = sources * stride
        chunk = math.gcd(total, 512)

        def widen(s, carry):
            part = pl.ds(pl.multiple_of(s * chunk, chunk), chunk)
            lift[part, :] = panel[part, :].astype(jnp.float32)
            return carry

        lax.fori_loop(0, total // chunk, widen, 0)

        def place(p, carry):
            to = pl.ds(pl.multiple_of(p * sources, sources), sources)
            if weighted:
                scale = weight_ref[pl.ds(band * WEIGHT_ROWS + p, sources, stride=FREQS * WEIGHT_ROWS), :]
            for j in range(groups):
                piece = lift[pl.ds(p * groups + j, sources, stride=stride), :]
                if weighted:
                    piece = piece * scale
                into[to, j * LANES : (j + 1) * LANES] = piece.astype(jnp.bfloat16)
            return carry

        lax.fori_loop(0, count, place, 0)

    @pl.when(at_tile == 0)
    def _():
        unpack(row_ref, left, False)
        unpack(col_ref, right, True)

    lhs = left[:, pl.ds(pl.multiple_of(at_tile * tile, tile), tile)]
    width = right.shape[1]
    step = math.gcd(width, 512)
    for at in range(0, width, step):
        out_ref[0, :, at : at + step] = lax.dot_general(
            lhs, right[:, at : at + step], (((0,), (0,)), ((), ())), preferred_element_type=jnp.float32
        )


def chi_block(row_panel, col_panel, weights, count, row_block, col_block):
    sources = weights.shape[0] // (FREQS * WEIGHT_ROWS)
    tile = math.gcd(row_block, 512)
    whole = lambda x: pl.BlockSpec(x.shape, lambda m: (0, 0), pipeline_mode=pl.Buffered(1))
    pairs = sources * count
    return pl.pallas_call(
        functools.partial(chi_kernel, count, tile),
        out_shape=jax.ShapeDtypeStruct((1, row_block, col_block), jnp.float32),
        grid=(row_block // tile,),
        in_specs=[whole(row_panel), whole(col_panel), whole(weights)],
        out_specs=pl.BlockSpec((1, tile, col_block), lambda m: (0, m, 0)),
        scratch_shapes=[
            pltpu.VMEM((max(row_panel.shape[0], col_panel.shape[0]), LANES), jnp.float32),
            pltpu.VMEM((pairs, row_block), jnp.bfloat16),
            pltpu.VMEM((pairs, col_block), jnp.bfloat16),
        ],
        compiler_params=pltpu.CompilerParams(vmem_limit_bytes=56 * 2**20),
        name="chi_block",
    )(row_panel, col_panel, weights)


def per_device(
    valence_orbitals,
    conduction_orbitals,
    valence_energy,
    conduction_energy,
    coulomb_root,
    pair_bands,
    slot_counts,
):
    grow_size = lax.axis_size("grow")
    gcol_size = lax.axis_size("gcol")
    factor = 1.0 / math.sqrt(2 * grow_size * gcol_size * SLOTS)
    half_slots = pair_bands.shape[1] // 2
    swap = [(0, 1), (1, 0)]

    con_own = conduction_orbitals.reshape(-1, M1, M2 * M3)
    con_other = lax.ppermute(con_own, "band", swap)
    own = jnp.concatenate([pair_bands.reshape(-1), slot_counts])
    other = lax.ppermute(own, "band", swap)
    band = lax.axis_index("band").astype(jnp.int32).reshape(1)
    density, weights = densities(
        valence_orbitals.reshape(-1, M1, M2 * M3), con_own, con_other, coulomb_root,
        own, other, band, valence_energy, conduction_energy, factor,
    )

    row_block = N1 * N2 * N3 // grow_size
    col_block = N1 * N2 * N3 // gcol_size

    def wire(blocks, block):
        parts = density.reshape(half_slots, blocks, block // LANES, LANES).transpose(1, 0, 2, 3)
        return parts.reshape(blocks, half_slots * (block // LANES), LANES)

    row_panel, col_panel, all_weights = exchange(
        wire(grow_size, row_block), wire(gcol_size, col_block), weights, grow_size, gcol_size
    )
    return chi_block(
        row_panel.reshape(-1, LANES),
        col_panel.reshape(-1, LANES),
        all_weights.reshape(-1, LANES),
        half_slots,
        row_block,
        col_block,
    )


def solution(mesh):
    return jax.shard_map(
        per_device,
        mesh=mesh,
        in_specs=(
            P(),
            P(("band", "grow", "gcol"), None),
            P(),
            P(),
            P(),
            P(None, ("band", "grow", "gcol")),
            P(("band", "grow", "gcol")),
        ),
        out_specs=P("band", "grow", "gcol"),
        check_vma=False,
    )
```
